256 devices in a mesh: blk: 16 (over x_hi, y, core), ab: 16 (over x_lo, z).
Axes of the slice: x: 4 (x_hi: 2, x_lo: 2; x = x_hi * 2 + x_lo), y: 4, z: 8, core: 2. Of those that a mesh axis runs over, the one named last changes fastest.
Arguments:
- amplitudes: bfloat16 [1024, 11264], P('blk'), may hold values from -6 to 6
- integrals: bfloat16 [32768, 11264], P(('blk', 'ab')), may hold values from -0.0546875 to 0.0546875
- live_rows: int32 [16], replicated, may hold values from 1 to 64, 640 in all
- partner: int32 [1024], replicated, may hold values from 0 to 1023, as said below
Outputs:
- ladder: float32 [1024, 32768], P(None, ('blk', 'ab'))
The draws below stay inside these ranges and needn't reach their ends.
Inputs may be any that keep to these rules, and one draw needn't show every extreme that they name: `live_rows`: lengths of the blocks; the largest equals 64. An involution without fixed points: partner[partner[r]] = r and partner[r] != r.
All inputs are finite; a program needn't handle non-finite values.
Results may differ from the reference program's by a relative error of at most 0.0003.
Values may be sent and summed in bfloat16 or wider, within the bound.
No kernel may reach another device: no remote copies, remote signals or barrier semaphores. Data moves between devices by JAX's collectives and lax.ppermute only.
A program may use at most 128 MiB of HBM per device.

```python
import math
import jax
import jax.numpy as jnp
import numpy as np
from jax import lax

CD = 11264
IJ_DEV = 64
AB_DEV = 128
BLOCKS = 16
IJ = 1024
AB = 32768
HALF = 1024
DEVICES = 256


def draw_partner(key, part):
    order = jax.random.permutation(key, IJ).astype(jnp.int32)
    paired = order.reshape(-1, 2)[:, ::-1].reshape(-1)
    return jnp.zeros((IJ,), jnp.int32).at[order].set(paired)


def level_of(key, dims, cuts, low, largest):
    def one(position, shards_of):
        steps = jax.random.uniform(jax.random.fold_in(jax.random.fold_in(key, 6), position), (shards_of,), jnp.float32, low / len(cuts), largest / len(cuts))
        return jnp.repeat(jnp.exp(steps), dims[position] // shards_of).reshape((-1,) + (1,) * (len(dims) - position - 1))

    gain = one(*cuts[0])
    for cut in cuts[1:]:
        gain = gain * one(*cut)
    return gain


def profile(count, total, limit, skew):
    loads = [(1 << 20) // math.isqrt(grade ** skew) + 1 for grade in range(2, count + 1)]
    spare, counts = total - limit - (count - 1), [1] * (count - 1)
    while spare > 0:
        free = [i for i in range(count - 1) if counts[i] < limit]
        mass, remaining = sum([loads[i] for i in free]), spare
        for i in free:
            extra = min(limit - counts[i], max(1, remaining * loads[i] // mass), spare)
            counts[i] = counts[i] + extra
            spare = spare - extra
    return np.array([limit] + counts)


def uneven(own_key, amount, total, limit, skew):
    if amount == 2:
        one = jax.random.randint(own_key, (), max(1, total - limit), min(limit, total - 1) + 1)
        return jnp.stack([one, total - one])
    lengths = jnp.asarray(profile(amount, total, limit, skew), jnp.int32)
    twos = (amount - 1) // 2
    source_of, sink = lengths[1:1 + 2 * twos:2], lengths[2:2 + 2 * twos:2]
    slack = jnp.minimum(source_of - 1, limit - sink)
    moved = jax.random.randint(jax.random.fold_in(own_key, 1), (twos,), 0, 1 << 20) % (slack + 1)
    lengths = lengths.at[1:1 + 2 * twos:2].set(source_of - moved).at[2:2 + 2 * twos:2].set(sink + moved)
    return lengths[jax.random.permutation(jax.random.fold_in(own_key, 2), amount)]


def noise(key, shape, width, most, pieces=(), held_as=jnp.bfloat16):
    drawn = width * jax.random.normal(key, shape, jnp.float32)
    if pieces:
        drawn = drawn * level_of(key, shape, pieces, -0.22, 0.18)
    return jnp.clip(drawn, -most, most).astype(held_as)


def setup_inputs(seed: int = 0) -> dict:
    key_list = jax.random.split(jax.random.key(seed), 5)
    return {
        "amplitudes": noise(key_list[0], (IJ, CD), 1.0, 6.0, ((0, 16),)),
        "integrals": noise(key_list[1], (AB, CD), CD ** -0.5, 0.0546875, ((0, 256),)),
        "live_rows": uneven(key_list[2], BLOCKS, IJ_DEV * BLOCKS * 5 // 8, IJ_DEV, 2).astype(jnp.int32),
        "partner": draw_partner(jax.random.fold_in(key_list[4], 71), 0),
    }


def reference(amplitudes, integrals, live_rows, partner):
    slots = jnp.arange(IJ, dtype=jnp.int32)
    live = (slots % IJ_DEV) < jnp.repeat(live_rows, IJ_DEV, total_repeat_length=IJ)
    blocks = integrals.reshape(DEVICES, AB_DEV, CD)

    def one_block(rows):
        return lax.dot_general(amplitudes, rows, (((1,), (1,)), ((), ())), preferred_element_type=jnp.float32)

    partial_w = lax.map(one_block, blocks)
    partial_w = jnp.transpose(partial_w, (1, 0, 2)).reshape(IJ, AB)
    partial_w = jnp.where(live[:, None], partial_w, jnp.zeros_like(partial_w))
    mated = partial_w.reshape(IJ, AB // (2 * HALF), 2, HALF)[:, :, ::-1, :].reshape(IJ, AB)
    return partial_w + mated[partner.astype(jnp.int32)]
```

```python
import jax
import jax.numpy as jnp
from jax import lax
from jax.experimental import pallas as pl
from jax.experimental.pallas import tpu as pltpu
from jax.sharding import PartitionSpec as P

AXES = ("blk", "ab")
NX, NY, NZ = 4, 4, 8


def place(x, y, z, c):
    return ((((x // 2) * NY + y) * 2 + c) * 2 + x % 2) * NZ + z


def other(i, n, odd):
    return (i ^ 1) if not odd else ((((i + 1) % n) ^ 1) - 1) % n


MOVES = {
    "x0": lambda x, y, z, c: (other(x, NX, 0), y, z, c),
    "x1": lambda x, y, z, c: (other(x, NX, 1), y, z, c),
    "y0": lambda x, y, z, c: (x, other(y, NY, 0), z, c),
    "y1": lambda x, y, z, c: (x, other(y, NY, 1), z, c),
    "core": lambda x, y, z, c: (x, y, z, c ^ 1),
}


def swap(block, move):
    pairs = [
        (place(x, y, z, c), place(*MOVES[move](x, y, z, c)))
        for x in range(NX) for y in range(NY) for z in range(NZ) for c in range(2)
    ]
    return lax.ppermute(block, AXES, pairs)


def dot_t(a, b):
    return lax.dot_general(a, b, (((1,), (1,)), ((), ())), preferred_element_type=jnp.float32)


def halves(t):
    high = t.astype(jnp.bfloat16)
    return high, (t - high.astype(jnp.float32)).astype(jnp.bfloat16)


def dot(a, b):
    return jnp.dot(a, b, preferred_element_type=jnp.float32)


def symmetrize_kernel(slot_ref, mate_slot_ref, own_ref, mate_ref, mine_ref, sibling_ref):
    rows = mine_ref.shape[0]
    r = lax.broadcasted_iota(jnp.int32, (rows, 1), 0) + pl.program_id(0) * rows
    direct = (r == slot_ref[...]).astype(jnp.bfloat16)
    crossed = (r == mate_slot_ref[...]).astype(jnp.bfloat16)
    mh, ml = halves(mate_ref[...])
    oh, ol = halves(own_ref[...])
    out = (dot(direct, mh) + dot(crossed, oh)) + (dot(direct, ml) + dot(crossed, ol))
    width = mine_ref.shape[1]
    mine_ref[...] = out[:, :width]
    sibling_ref[...] = out[:, width:]


def symmetrize(slot, mate_slot, own, mate, total):
    n, w = own.shape
    rows = 256
    whole = lambda shape: pl.BlockSpec(shape, lambda i: (0, 0))
    return pl.pallas_call(
        symmetrize_kernel,
        grid=(total // rows,),
        in_specs=[whole((1, n)), whole((1, n)), whole((n, w)), whole((n, w))],
        out_specs=[pl.BlockSpec((rows, w // 2), lambda i: (i, 0))] * 2,
        out_shape=[jax.ShapeDtypeStruct((total, w // 2), jnp.float32)] * 2,
        compiler_params=pltpu.CompilerParams(vmem_limit_bytes=48 << 20),
        name="symmetrize",
    )(slot, mate_slot, own, mate)


def reorder_kernel(partner_ref, t_ref, o_ref):
    rows, n = o_ref.shape[0], t_ref.shape[0]
    pick = (partner_ref[...] == lax.broadcasted_iota(jnp.int32, (rows, n), 1)).astype(jnp.bfloat16)
    high, low = halves(t_ref[...])
    o_ref[...] = dot(pick, high) + dot(pick, low)


def reorder(partner, t):
    n, w = t.shape
    rows = 256
    return pl.pallas_call(
        reorder_kernel,
        grid=(n // rows,),
        in_specs=[pl.BlockSpec((rows, 1), lambda i: (i, 0)), pl.BlockSpec((n, w), lambda i: (0, 0))],
        out_specs=pl.BlockSpec((rows, w), lambda i: (i, 0)),
        out_shape=jax.ShapeDtypeStruct((n, w), jnp.float32),
        compiler_params=pltpu.CompilerParams(vmem_limit_bytes=48 << 20),
        name="reorder",
    )(partner[:, None], t)


def shards(amplitudes, integrals, live_rows, partner):
    height, depth = amplitudes.shape
    total = partner.shape[0]
    half = depth // 2
    blk, ab = lax.axis_index("blk"), lax.axis_index("ab")
    xh, y, c = blk // (2 * NY), (blk // 2) % NY, blk % 2
    xl = ab // NZ
    upper = (xh ^ xl) == 1
    keep = lambda t: jnp.where(upper, t[:, half:], t[:, :half])
    give = lambda t: jnp.where(upper, t[:, :half], t[:, half:])

    b_mine = keep(integrals)
    b_mate = swap(give(integrals), "x0")
    u = {"": keep(amplitudes)}
    u["a"] = swap(u[""], "x1")
    u["b"] = swap(u[""], "y0")
    u["c"] = swap(u[""], "y1")
    b_sib = swap(b_mine, "core")
    u["ab"] = swap(u["b"], "x1")
    u["bc"] = swap(u["c"], "y0")
    u["ac"] = swap(u["a"], "y1")
    cuts = [0, half * 15 // 44 // 128 * 128, half * 30 // 44 // 128 * 128, half]
    part = lambda t, i: t[:, cuts[i]:cuts[i + 1]]
    u["abc"] = jnp.concatenate(
        [swap(part(u["bc"], 0), "x1"), swap(part(u["ac"], 1), "y0"), swap(part(u["ab"], 2), "y1")], axis=1)
    b_mate_sib = swap(b_mate, "core")

    order = ["", "a", "b", "c", "ab", "bc", "ac", "abc"]
    groups = [order[:4], order[4:7], order[7:]]
    own, mate = [], []
    b_own = jnp.concatenate([b_mine, b_sib], axis=0)
    b_far = jnp.concatenate([b_mate, b_mate_sib], axis=0)
    for names in groups:
        rows = jnp.concatenate([u[n] for n in names], axis=0)
        own.append(dot_t(rows, b_own))
        mate.append(dot_t(rows, b_far))
    own, mate = jnp.concatenate(own, axis=0), jnp.concatenate(mate, axis=0)

    blocks = []
    for n in order:
        xh_n = xh ^ 1 if "a" in n else xh
        y_n = y
        if "b" in n:
            y_n = y_n ^ 1
        if "c" in n:
            y_n = (((y_n + 1) ^ 1) - 1) % NY
        blocks.append((xh_n * NY + y_n) * 2 + c)
    blocks = jnp.stack(blocks)
    lane = jnp.arange(height, dtype=jnp.int32)
    slot = (blocks[:, None] * height + lane[None, :]).reshape(-1)
    alive = (lane[None, :] < live_rows[blocks][:, None]).reshape(-1)
    mate_slot = jnp.where(alive, partner[slot], -1)[None, :]
    slot = jnp.where(alive, slot, -1)[None, :]

    mine, sibling = symmetrize(slot, mate_slot, own, mate, total)
    mine = mine + swap(sibling, "core")
    return swap(mine, "x0") + reorder(partner, mine)


def solution(mesh):
    return jax.shard_map(
        shards,
        mesh=mesh,
        in_specs=(P("blk", None), P(("blk", "ab"), None), P(), P()),
        out_specs=P(None, ("blk", "ab")),
        check_vma=False,
    )
```

```python
import jax
import jax.numpy as jnp
from jax import lax
from jax.experimental import pallas as pl
from jax.experimental.pallas import tpu as pltpu
from jax.sharding import PartitionSpec as P

AXES = ("blk", "ab")
NX, NY, NZ = 4, 4, 8
ROOM = pltpu.CompilerParams(vmem_limit_bytes=16 << 20)
ANYWHERE = pl.BlockSpec(memory_space=pl.ANY)
WHOLE = pl.BlockSpec(memory_space=pltpu.VMEM)


def place(x, y, z, c):
    return ((((x // 2) * NY + y) * 2 + c) * 2 + x % 2) * NZ + z


def other(i, n, odd):
    return ((((i + 1) % n) ^ 1) - 1) % n if odd else i ^ 1


MOVES = {
    "x0": lambda x, y, z, c: (other(x, NX, 0), y, z, c),
    "x1": lambda x, y, z, c: (other(x, NX, 1), y, z, c),
    "y0": lambda x, y, z, c: (x, other(y, NY, 0), z, c),
    "y1": lambda x, y, z, c: (x, other(y, NY, 1), z, c),
    "core": lambda x, y, z, c: (x, y, z, c ^ 1),
}


def swap(block, move):
    pairs = [
        (place(x, y, z, c), place(*MOVES[move](x, y, z, c)))
        for x in range(NX) for y in range(NY) for z in range(NZ) for c in range(2)
    ]
    return lax.ppermute(block, AXES, pairs)


def dot_t(a, b):
    return lax.dot_general(a, b, (((1,), (1,)), ((), ())), preferred_element_type=jnp.float32)


def dot(a, b):
    return jnp.dot(a, b, preferred_element_type=jnp.float32)


def halves(t):
    high = t.astype(jnp.bfloat16)
    return high, (t - high.astype(jnp.float32)).astype(jnp.bfloat16)


def cost(us):
    return pl.CostEstimate(flops=int(us * 1e9), bytes_accessed=int(us * 3e6), transcendentals=0)


def tied(value, *before):
    return lax.optimization_barrier((value, *before))[0]


def columns(ref, which, width):
    return ref.at[:, pl.ds(pl.multiple_of(which * width, width), width)]


def split_kernel(which_ref, a_ref, b_ref, keep_ref, give_ref, sem):
    width = keep_ref.shape[1]
    which = which_ref[0]
    keep = pltpu.make_async_copy(columns(a_ref, which, width), keep_ref, sem.at[0])
    give = pltpu.make_async_copy(columns(b_ref, 1 - which, width), give_ref, sem.at[1])
    keep.start()
    give.start()
    keep.wait()
    give.wait()


def split(which, a, b):
    half = a.shape[1] // 2
    return pl.pallas_call(
        split_kernel,
        in_specs=[pl.BlockSpec(memory_space=pltpu.SMEM), ANYWHERE, ANYWHERE],
        out_specs=[WHOLE, WHOLE],
        out_shape=[jax.ShapeDtypeStruct((t.shape[0], half), t.dtype) for t in (a, b)],
        scratch_shapes=[pltpu.SemaphoreType.DMA((2,))],
        cost_estimate=cost(2),
        name="split",
    )(which, a, b)


def first_kernel(n, which_ref, mine_ref, sibling_ref, *refs):
    rows, t_ref, cols_ref, held_ref, sem = refs[:n], *refs[n:]
    width = cols_ref.shape[1]
    high = mine_ref.shape[0]
    low = rows[0].shape[0]
    copies = [
        pltpu.make_async_copy(columns(mine_ref, which_ref[0], width), cols_ref.at[pl.ds(0, high)], sem.at[n]),
        pltpu.make_async_copy(columns(sibling_ref, which_ref[0], width), cols_ref.at[pl.ds(high, high)], sem.at[n + 1]),
    ] + [pltpu.make_async_copy(r, held_ref.at[pl.ds(i * low, low)], sem.at[i]) for i, r in enumerate(rows)]
    for copy in copies:
        copy.start()
    for copy in copies:
        copy.wait()
    t_ref[...] = dot_t(held_ref[...], cols_ref[...])


def first_product(which, mine, sibling, rows):
    n, high = len(rows), mine.shape[0]
    low, width = rows[0].shape
    return pl.pallas_call(
        lambda *refs: first_kernel(n, *refs),
        in_specs=[pl.BlockSpec(memory_space=pltpu.SMEM)] + [ANYWHERE] * (2 + n),
        out_specs=[WHOLE] * 3,
        out_shape=[
            jax.ShapeDtypeStruct((n * low, 2 * high), jnp.float32),
            jax.ShapeDtypeStruct((2 * high, width), mine.dtype),
            jax.ShapeDtypeStruct((n * low, width), mine.dtype),
        ],
        scratch_shapes=[pltpu.SemaphoreType.DMA((n + 2,))],
        compiler_params=ROOM,
        cost_estimate=cost(3),
        name="first_product",
    )(which, mine, sibling, *rows)


def pack_kernel(n, *refs):
    rows, out_ref, sem = refs[:n], *refs[n:]
    low = rows[0].shape[0]
    copies = [pltpu.make_async_copy(r, out_ref.at[pl.ds(i * low, low)], sem.at[i]) for i, r in enumerate(rows)]
    for copy in copies:
        copy.start()
    for copy in copies:
        copy.wait()


def pack(rows):
    n = len(rows)
    low, width = rows[0].shape
    return pl.pallas_call(
        lambda *refs: pack_kernel(n, *refs),
        in_specs=[ANYWHERE] * n,
        out_specs=WHOLE,
        out_shape=jax.ShapeDtypeStruct((n * low, width), rows[0].dtype),
        scratch_shapes=[pltpu.SemaphoreType.DMA((n,))],
        compiler_params=ROOM,
        cost_estimate=cost(2),
        name="pack",
    )(*rows)


def spread(slot_ref, partner_ref):
    r = lax.broadcasted_iota(jnp.int32, partner_ref.shape, 0)
    direct = (r == slot_ref[...]).astype(jnp.bfloat16)
    crossed = (partner_ref[...] == slot_ref[...]).astype(jnp.bfloat16)
    return direct, crossed


def symmetrize_kernel(n, slot_ref, partner_ref, *refs):
    own = jnp.concatenate([r[...] for r in refs[:n]], axis=0)
    mate = jnp.concatenate([r[...] for r in refs[n:2 * n]], axis=0)
    mine_ref, sibling_ref, largest_ref = refs[2 * n:]
    direct, crossed = spread(slot_ref, partner_ref)
    mh, ml = halves(mate)
    oh, ol = halves(own)
    out = (dot(direct, mh) + dot(crossed, oh)) + (dot(direct, ml) + dot(crossed, ol))
    total, width = mine_ref.shape
    mine, sibling = out[:, :width], out[:, width:]
    mine_ref[...] = mine
    sibling_ref[:total] = sibling
    largest_ref[...] = jnp.full(largest_ref.shape, jnp.max(jnp.abs(mine)))
    sibling_ref[total:] = jnp.full(largest_ref.shape, jnp.max(jnp.abs(sibling)))


def symmetrize(slot, partner, own, mate):
    total, width = partner.shape[0], own[0].shape[1] // 2
    return pl.pallas_call(
        lambda *refs: symmetrize_kernel(len(own), *refs),
        out_shape=[jax.ShapeDtypeStruct((n, width), jnp.float32) for n in (total, total + 8, 8)],
        compiler_params=ROOM,
        cost_estimate=cost(2),
        name="symmetrize",
    )(slot, partner, *own, *mate)


def reorder_kernel(partner_ref, t_ref, o_ref):
    n = t_ref.shape[0]
    pick = (partner_ref[...] == lax.broadcasted_iota(jnp.int32, (n, n), 1)).astype(jnp.bfloat16)
    high, low = halves(t_ref[...])
    o_ref[...] = dot(pick, high) + dot(pick, low)


def reorder(partner, t):
    return pl.pallas_call(
        reorder_kernel,
        out_shape=jax.ShapeDtypeStruct(t.shape, jnp.float32),
        compiler_params=ROOM,
        cost_estimate=cost(2),
        name="reorder",
    )(partner, t)


def shards(amplitudes, integrals, live_rows, partner):
    height, depth = amplitudes.shape
    total = partner.shape[0]
    half = depth // 2
    blk, ab = lax.axis_index("blk"), lax.axis_index("ab")
    xh, y, c = blk // (2 * NY), (blk // 2) % NY, blk % 2
    which = (xh ^ (ab // NZ)).astype(jnp.int32)[None]
    partner = partner[:, None]

    names = ["", "a", "b", "c", "ab", "bc", "ac", "abc"]
    blocks = []
    for n in names:
        xh_n, y_n = (xh ^ 1 if "a" in n else xh), y
        if "b" in n:
            y_n = y_n ^ 1
        if "c" in n:
            y_n = (((y_n + 1) ^ 1) - 1) % NY
        blocks.append((xh_n * NY + y_n) * 2 + c)
    blocks = jnp.stack(blocks)
    lane = jnp.arange(height, dtype=jnp.int32)
    alive = lane[None, :] < live_rows[blocks][:, None]
    slot = jnp.where(alive, blocks[:, None] * height + lane[None, :], -1).reshape(1, -1)

    u = {}
    u[""], given = split(which, amplitudes, integrals)
    u["a"] = swap(u[""], "x1")
    u["b"] = swap(u[""], "y0")
    u["c"] = swap(u[""], "y1")
    b_mate = swap(given, "x0")
    b_sib = swap(integrals, "core")
    u["ab"] = swap(u["b"], "x1")
    u["bc"] = swap(u["c"], "y0")
    u["ac"] = swap(u["a"], "y1")
    rows = [u[n] for n in names[:7]]
    which, slot, partner = lax.optimization_barrier((which, slot, partner))
    own_first, b_own, first = first_product(which, integrals, b_sib, rows[:4])
    cuts = [0, half * 15 // 44 // 128 * 128, half * 30 // 44 // 128 * 128, half]
    cut = [u[n][:, cuts[i]:cuts[i + 1]] for i, n in enumerate(("bc", "ac", "ab"))]
    last = jnp.concatenate([swap(t, move) for t, move in zip(cut, ("x1", "y0", "y1"))], axis=1)
    b_mate = tied(b_mate, *cut)
    b_mate_sib = swap(b_mate, "core")
    second = pack(rows[4:])
    own = [own_first, dot_t(second, b_own), dot_t(last, b_own)]
    b_far = jnp.concatenate([b_mate, b_mate_sib], axis=0)
    mate = [dot_t(t, b_far) for t in (first, second, last)]
    mine, sibling, largest = symmetrize(slot, partner, own, mate)
    sibling = swap(sibling, "core")
    mine = mine + sibling[:total]
    bound = largest[:1] + sibling[total:total + 1]
    power = jnp.clip(14.0 - jnp.ceil(jnp.log2(jnp.maximum(bound, 1e-37))), -120.0, 120.0)
    sent = jnp.concatenate(
        [(mine * jnp.exp2(power)).astype(jnp.float16), jnp.broadcast_to(power.astype(jnp.float16), (16, mine.shape[1]))],
        axis=0)
    came = swap(sent, "x0")
    scale = jnp.exp2(-came[total:total + 1].astype(jnp.float32))
    return came[:total].astype(jnp.float32) * scale + reorder(partner, mine)


def solution(mesh):
    return jax.shard_map(
        shards,
        mesh=mesh,
        in_specs=(P("blk", None), P(("blk", "ab"), None), P(), P()),
        out_specs=P(None, ("blk", "ab")),
        check_vma=False,
    )
```

```python
import jax
import jax.numpy as jnp
from jax import lax
from jax.experimental import pallas as pl
from jax.experimental.pallas import tpu as pltpu
from jax.sharding import PartitionSpec as P

AXES = ("blk", "ab")
NX, NY, NZ = 4, 4, 8
ROOM = pltpu.CompilerParams(vmem_limit_bytes=16 << 20)
ANYWHERE = pl.BlockSpec(memory_space=pl.ANY)
WHOLE = pl.BlockSpec(memory_space=pltpu.VMEM)


def place(x, y, z, c):
    return ((((x // 2) * NY + y) * 2 + c) * 2 + x % 2) * NZ + z


def other(i, n, odd):
    return ((((i + 1) % n) ^ 1) - 1) % n if odd else i ^ 1


MOVES = {
    "x0": lambda x, y, z, c: (other(x, NX, 0), y, z, c),
    "x1": lambda x, y, z, c: (other(x, NX, 1), y, z, c),
    "y0": lambda x, y, z, c: (x, other(y, NY, 0), z, c),
    "y1": lambda x, y, z, c: (x, other(y, NY, 1), z, c),
    "core": lambda x, y, z, c: (x, y, z, c ^ 1),
}


def swap(block, move):
    pairs = [
        (place(x, y, z, c), place(*MOVES[move](x, y, z, c)))
        for x in range(NX) for y in range(NY) for z in range(NZ) for c in range(2)
    ]
    return lax.ppermute(block, AXES, pairs)


def dot_t(a, b):
    return lax.dot_general(a, b, (((1,), (1,)), ((), ())), preferred_element_type=jnp.float32)


def dot(a, b):
    return jnp.dot(a, b, preferred_element_type=jnp.float32)


def halves(t):
    high = t.astype(jnp.bfloat16)
    return high, (t - high.astype(jnp.float32)).astype(jnp.bfloat16)


def cost(us):
    return pl.CostEstimate(flops=int(us * 1e9), bytes_accessed=int(us * 3e6), transcendentals=0)


def tied(value, *before):
    return lax.optimization_barrier((value, *before))[0]


def columns(ref, which, width):
    return ref.at[:, pl.ds(pl.multiple_of(which * width, width), width)]


def half_kernel(which_ref, source_ref, out_ref, sem):
    copy = pltpu.make_async_copy(columns(source_ref, which_ref[0], out_ref.shape[1]), out_ref, sem)
    copy.start()
    copy.wait()


def half_of(which, table):
    return pl.pallas_call(
        half_kernel,
        in_specs=[pl.BlockSpec(memory_space=pltpu.SMEM), ANYWHERE],
        out_specs=WHOLE,
        out_shape=jax.ShapeDtypeStruct((table.shape[0], table.shape[1] // 2), table.dtype),
        scratch_shapes=[pltpu.SemaphoreType.DMA],
        cost_estimate=cost(2),
        name="half",
    )(which, table)


def first_kernel(n, which_ref, mine_ref, sibling_ref, *refs):
    rows, t_ref, cols_ref, held_ref, sem = refs[:n], *refs[n:]
    width = cols_ref.shape[1]
    high = mine_ref.shape[0]
    low = rows[0].shape[0]
    copies = [
        pltpu.make_async_copy(columns(mine_ref, which_ref[0], width), cols_ref.at[pl.ds(0, high)], sem.at[n]),
        pltpu.make_async_copy(columns(sibling_ref, which_ref[0], width), cols_ref.at[pl.ds(high, high)], sem.at[n + 1]),
    ] + [pltpu.make_async_copy(r, held_ref.at[pl.ds(i * low, low)], sem.at[i]) for i, r in enumerate(rows)]
    for copy in copies:
        copy.start()
    for copy in copies:
        copy.wait()
    t_ref[...] = dot_t(held_ref[...], cols_ref[...])


def first_product(which, mine, sibling, rows):
    n, high = len(rows), mine.shape[0]
    low, width = rows[0].shape
    return pl.pallas_call(
        lambda *refs: first_kernel(n, *refs),
        in_specs=[pl.BlockSpec(memory_space=pltpu.SMEM)] + [ANYWHERE] * (2 + n),
        out_specs=[WHOLE] * 3,
        out_shape=[
            jax.ShapeDtypeStruct((n * low, 2 * high), jnp.float32),
            jax.ShapeDtypeStruct((2 * high, width), mine.dtype),
            jax.ShapeDtypeStruct((n * low, width), mine.dtype),
        ],
        scratch_shapes=[pltpu.SemaphoreType.DMA((n + 2,))],
        compiler_params=ROOM,
        cost_estimate=cost(3),
        name="first_product",
    )(which, mine, sibling, *rows)


def pack_kernel(n, *refs):
    rows, out_ref, sem = refs[:n], *refs[n:]
    low = rows[0].shape[0]
    copies = [pltpu.make_async_copy(r, out_ref.at[pl.ds(i * low, low)], sem.at[i]) for i, r in enumerate(rows)]
    for copy in copies:
        copy.start()
    for copy in copies:
        copy.wait()


def pack(rows):
    n = len(rows)
    low, width = rows[0].shape
    return pl.pallas_call(
        lambda *refs: pack_kernel(n, *refs),
        in_specs=[ANYWHERE] * n,
        out_specs=WHOLE,
        out_shape=jax.ShapeDtypeStruct((n * low, width), rows[0].dtype),
        scratch_shapes=[pltpu.SemaphoreType.DMA((n,))],
        compiler_params=ROOM,
        cost_estimate=cost(2),
        name="pack",
    )(*rows)


def spread(slot_ref, partner_ref):
    r = lax.broadcasted_iota(jnp.int32, partner_ref.shape, 0)
    direct = (r == slot_ref[...]).astype(jnp.bfloat16)
    crossed = (partner_ref[...] == slot_ref[...]).astype(jnp.bfloat16)
    return direct, crossed


def symmetrize_kernel(n, slot_ref, partner_ref, *refs):
    own = jnp.concatenate([r[...] for r in refs[:n]], axis=0)
    mate = jnp.concatenate([r[...] for r in refs[n:2 * n]], axis=0)
    mine_ref, sibling_ref, largest_ref = refs[2 * n:]
    direct, crossed = spread(slot_ref, partner_ref)
    mh, ml = halves(mate)
    oh, ol = halves(own)
    out = (dot(direct, mh) + dot(crossed, oh)) + (dot(direct, ml) + dot(crossed, ol))
    total, width = mine_ref.shape
    mine, sibling = out[:, :width], out[:, width:]
    mine_ref[...] = mine
    sibling_ref[:total] = sibling
    largest_ref[...] = jnp.full(largest_ref.shape, jnp.max(jnp.abs(mine)))
    sibling_ref[total:] = jnp.full(largest_ref.shape, jnp.max(jnp.abs(sibling)))


def symmetrize(slot, partner, own, mate):
    total, width = partner.shape[0], own[0].shape[1] // 2
    return pl.pallas_call(
        lambda *refs: symmetrize_kernel(len(own), *refs),
        out_shape=[jax.ShapeDtypeStruct((n, width), jnp.float32) for n in (total, total + 8, 8)],
        compiler_params=ROOM,
        cost_estimate=cost(2),
        name="symmetrize",
    )(slot, partner, *own, *mate)


def reorder_kernel(partner_ref, t_ref, o_ref):
    n = t_ref.shape[0]
    pick = (partner_ref[...] == lax.broadcasted_iota(jnp.int32, (n, n), 1)).astype(jnp.bfloat16)
    high, low = halves(t_ref[...])
    o_ref[...] = dot(pick, high) + dot(pick, low)


def reorder(partner, t):
    return pl.pallas_call(
        reorder_kernel,
        out_shape=jax.ShapeDtypeStruct(t.shape, jnp.float32),
        compiler_params=ROOM,
        cost_estimate=cost(2),
        name="reorder",
    )(partner, t)


def shards(amplitudes, integrals, live_rows, partner):
    height, depth = amplitudes.shape
    total = partner.shape[0]
    half = depth // 2
    blk, ab = lax.axis_index("blk"), lax.axis_index("ab")
    xh, y, c = blk // (2 * NY), (blk // 2) % NY, blk % 2
    which = (xh ^ (ab // NZ)).astype(jnp.int32)[None]
    partner = partner[:, None]

    names = ["", "a", "b", "c", "ab", "bc", "ac", "abc"]
    blocks = []
    for n in names:
        xh_n, y_n = (xh ^ 1 if "a" in n else xh), y
        if "b" in n:
            y_n = y_n ^ 1
        if "c" in n:
            y_n = (((y_n + 1) ^ 1) - 1) % NY
        blocks.append((xh_n * NY + y_n) * 2 + c)
    blocks = jnp.stack(blocks)
    lane = jnp.arange(height, dtype=jnp.int32)
    alive = lane[None, :] < live_rows[blocks][:, None]
    slot = jnp.where(alive, blocks[:, None] * height + lane[None, :], -1).reshape(1, -1)

    u = {}
    u[""] = jnp.where(which[0] == 1, amplitudes[:, half:], amplitudes[:, :half])
    given = half_of(1 - which, tied(integrals, u[""]))
    u["a"] = swap(u[""], "x1")
    u["b"] = swap(u[""], "y0")
    u["c"] = swap(u[""], "y1")
    b_mate = swap(given, "x0")
    b_sib = swap(integrals, "core")
    u["ab"] = swap(u["b"], "x1")
    u["bc"] = swap(u["c"], "y0")
    u["ac"] = swap(u["a"], "y1")
    rows = [u[n] for n in names[:7]]
    which, slot, partner = lax.optimization_barrier((which, slot, partner))
    own_first, b_own, first = first_product(which, integrals, b_sib, rows[:4])
    cuts = [0, half * 15 // 44 // 128 * 128, half * 30 // 44 // 128 * 128, half]
    cut = [tied(u[n], own_first)[:, cuts[i]:cuts[i + 1]] for i, n in enumerate(("bc", "ac", "ab"))]
    last = jnp.concatenate([swap(t, move) for t, move in zip(cut, ("x1", "y0", "y1"))], axis=1)
    b_mate = tied(b_mate, *cut)
    b_mate_sib = swap(b_mate, "core")
    second = pack([tied(r, *cut) for r in rows[4:]])
    own = [own_first, dot_t(second, b_own), dot_t(last, b_own)]
    b_far = jnp.concatenate([b_mate, b_mate_sib], axis=0)
    mate = [dot_t(t, b_far) for t in (first, second, last)]
    mine, sibling, largest = symmetrize(slot, partner, own, mate)
    sibling = swap(sibling, "core")
    mine = mine + sibling[:total]
    bound = largest[:1] + sibling[total:total + 1]
    power = jnp.clip(14.0 - jnp.ceil(jnp.log2(jnp.maximum(bound, 1e-37))), -120.0, 120.0)
    sent = jnp.concatenate(
        [(mine * jnp.exp2(power)).astype(jnp.float16), jnp.broadcast_to(power.astype(jnp.float16), (16, mine.shape[1]))],
        axis=0)
    came = swap(sent, "x0")
    scale = jnp.exp2(-came[total:total + 1].astype(jnp.float32))
    return came[:total].astype(jnp.float32) * scale + reorder(partner, mine)


def solution(mesh):
    return jax.shard_map(
        shards,
        mesh=mesh,
        in_specs=(P("blk", None), P(("blk", "ab"), None), P(), P()),
        out_specs=P(None, ("blk", "ab")),
        check_vma=False,
    )
```

```python
import jax
import jax.numpy as jnp
from jax import lax
from jax.experimental import pallas as pl
from jax.experimental.pallas import tpu as pltpu
from jax.sharding import PartitionSpec as P

AXES = ("blk", "ab")
NX, NY, NZ = 4, 4, 8
ROOM = pltpu.CompilerParams(vmem_limit_bytes=16 << 20)
ANYWHERE = pl.BlockSpec(memory_space=pl.ANY)
WHOLE = pl.BlockSpec(memory_space=pltpu.VMEM)


def place(x, y, z, c):
    return ((((x // 2) * NY + y) * 2 + c) * 2 + x % 2) * NZ + z


def other(i, n, odd):
    return ((((i + 1) % n) ^ 1) - 1) % n if odd else i ^ 1


MOVES = {
    "x0": lambda x, y, z, c: (other(x, NX, 0), y, z, c),
    "x1": lambda x, y, z, c: (other(x, NX, 1), y, z, c),
    "y0": lambda x, y, z, c: (x, other(y, NY, 0), z, c),
    "y1": lambda x, y, z, c: (x, other(y, NY, 1), z, c),
    "core": lambda x, y, z, c: (x, y, z, c ^ 1),
}


def swap(block, move):
    pairs = [
        (place(x, y, z, c), place(*MOVES[move](x, y, z, c)))
        for x in range(NX) for y in range(NY) for z in range(NZ) for c in range(2)
    ]
    return lax.ppermute(block, AXES, pairs)


def dot_t(a, b):
    return lax.dot_general(a, b, (((1,), (1,)), ((), ())), preferred_element_type=jnp.float32)


def dot(a, b):
    return jnp.dot(a, b, preferred_element_type=jnp.float32)


def halves(t):
    high = t.astype(jnp.bfloat16)
    return high, (t - high.astype(jnp.float32)).astype(jnp.bfloat16)


def cost(us):
    return pl.CostEstimate(flops=int(us * 1e9), bytes_accessed=int(us * 3e6), transcendentals=0)


def tied(value, *before):
    return lax.optimization_barrier((value, *before))[0]


def columns(ref, which, width):
    return ref.at[:, pl.ds(pl.multiple_of(which * width, width), width)]


def half_kernel(which_ref, source_ref, out_ref, sem):
    copy = pltpu.make_async_copy(columns(source_ref, which_ref[0], out_ref.shape[1]), out_ref, sem)
    copy.start()
    copy.wait()


def half_of(which, table):
    return pl.pallas_call(
        half_kernel,
        in_specs=[pl.BlockSpec(memory_space=pltpu.SMEM), ANYWHERE],
        out_specs=WHOLE,
        out_shape=jax.ShapeDtypeStruct((table.shape[0], table.shape[1] // 2), table.dtype),
        scratch_shapes=[pltpu.SemaphoreType.DMA],
        cost_estimate=cost(2),
        name="half",
    )(which, table)


def first_kernel(n, which_ref, mine_ref, sibling_ref, *refs):
    rows, t_ref, cols_ref, held_ref, sem = refs[:n], *refs[n:]
    width = cols_ref.shape[1]
    high = mine_ref.shape[0]
    low = rows[0].shape[0]
    copies = [
        pltpu.make_async_copy(columns(mine_ref, which_ref[0], width), cols_ref.at[pl.ds(0, high)], sem.at[n]),
        pltpu.make_async_copy(columns(sibling_ref, which_ref[0], width), cols_ref.at[pl.ds(high, high)], sem.at[n + 1]),
    ] + [pltpu.make_async_copy(r, held_ref.at[pl.ds(i * low, low)], sem.at[i]) for i, r in enumerate(rows)]
    for copy in copies:
        copy.start()
    for copy in copies:
        copy.wait()
    t_ref[...] = dot_t(held_ref[...], cols_ref[...])


def first_product(which, mine, sibling, rows):
    n, high = len(rows), mine.shape[0]
    low, width = rows[0].shape
    return pl.pallas_call(
        lambda *refs: first_kernel(n, *refs),
        in_specs=[pl.BlockSpec(memory_space=pltpu.SMEM)] + [ANYWHERE] * (2 + n),
        out_specs=[WHOLE] * 3,
        out_shape=[
            jax.ShapeDtypeStruct((n * low, 2 * high), jnp.float32),
            jax.ShapeDtypeStruct((2 * high, width), mine.dtype),
            jax.ShapeDtypeStruct((n * low, width), mine.dtype),
        ],
        scratch_shapes=[pltpu.SemaphoreType.DMA((n + 2,))],
        compiler_params=ROOM,
        cost_estimate=cost(3),
        name="first_product",
    )(which, mine, sibling, *rows)


def pack_kernel(n, *refs):
    rows, out_ref, sem = refs[:n], *refs[n:]
    low = rows[0].shape[0]
    copies = [pltpu.make_async_copy(r, out_ref.at[pl.ds(i * low, low)], sem.at[i]) for i, r in enumerate(rows)]
    for copy in copies:
        copy.start()
    for copy in copies:
        copy.wait()


def pack(rows):
    n = len(rows)
    low, width = rows[0].shape
    return pl.pallas_call(
        lambda *refs: pack_kernel(n, *refs),
        in_specs=[ANYWHERE] * n,
        out_specs=WHOLE,
        out_shape=jax.ShapeDtypeStruct((n * low, width), rows[0].dtype),
        scratch_shapes=[pltpu.SemaphoreType.DMA((n,))],
        compiler_params=ROOM,
        cost_estimate=cost(2),
        name="pack",
    )(*rows)


def spread(slot_ref, partner_ref):
    r = lax.broadcasted_iota(jnp.int32, partner_ref.shape, 0)
    direct = (r == slot_ref[...]).astype(jnp.bfloat16)
    crossed = (partner_ref[...] == slot_ref[...]).astype(jnp.bfloat16)
    return direct, crossed


def symmetrize_kernel(n, slot_ref, partner_ref, *refs):
    own = jnp.concatenate([r[...] for r in refs[:n]], axis=0)
    mate = jnp.concatenate([r[...] for r in refs[n:2 * n]], axis=0)
    mine_ref, sibling_ref, largest_ref = refs[2 * n:]
    direct, crossed = spread(slot_ref, partner_ref)
    mh, ml = halves(mate)
    oh, ol = halves(own)
    out = (dot(direct, mh) + dot(crossed, oh)) + (dot(direct, ml) + dot(crossed, ol))
    total, width = mine_ref.shape
    mine, sibling = out[:, :width], out[:, width:]
    mine_ref[...] = mine
    sibling_ref[:total] = sibling
    largest_ref[...] = jnp.full(largest_ref.shape, jnp.max(jnp.abs(mine)))
    sibling_ref[total:] = jnp.full(largest_ref.shape, jnp.max(jnp.abs(sibling)))


def symmetrize(slot, partner, own, mate):
    total, width = partner.shape[0], own[0].shape[1] // 2
    return pl.pallas_call(
        lambda *refs: symmetrize_kernel(len(own), *refs),
        out_shape=[jax.ShapeDtypeStruct((n, width), jnp.float32) for n in (total, total + 8, 8)],
        compiler_params=ROOM,
        cost_estimate=cost(2),
        name="symmetrize",
    )(slot, partner, *own, *mate)


def reorder_kernel(partner_ref, t_ref, o_ref):
    n = t_ref.shape[0]
    pick = (partner_ref[...] == lax.broadcasted_iota(jnp.int32, (n, n), 1)).astype(jnp.bfloat16)
    high, low = halves(t_ref[...])
    o_ref[...] = dot(pick, high) + dot(pick, low)


def reorder(partner, t):
    return pl.pallas_call(
        reorder_kernel,
        out_shape=jax.ShapeDtypeStruct(t.shape, jnp.float32),
        compiler_params=ROOM,
        cost_estimate=cost(2),
        name="reorder",
    )(partner, t)


def shards(amplitudes, integrals, live_rows, partner):
    height, depth = amplitudes.shape
    total = partner.shape[0]
    half = depth // 2
    blk, ab = lax.axis_index("blk"), lax.axis_index("ab")
    xh, y, c = blk // (2 * NY), (blk // 2) % NY, blk % 2
    which = (xh ^ (ab // NZ)).astype(jnp.int32)[None]
    partner = partner[:, None]

    names = ["", "a", "b", "c", "ab", "bc", "ac", "abc"]
    blocks = []
    for n in names:
        xh_n, y_n = (xh ^ 1 if "a" in n else xh), y
        if "b" in n:
            y_n = y_n ^ 1
        if "c" in n:
            y_n = (((y_n + 1) ^ 1) - 1) % NY
        blocks.append((xh_n * NY + y_n) * 2 + c)
    blocks = jnp.stack(blocks)
    lane = jnp.arange(height, dtype=jnp.int32)
    alive = lane[None, :] < live_rows[blocks][:, None]
    slot = jnp.where(alive, blocks[:, None] * height + lane[None, :], -1).reshape(1, -1)

    u = {}
    u[""] = jnp.where(which[0] == 1, amplitudes[:, half:], amplitudes[:, :half])
    given = half_of(1 - which, tied(integrals, u[""]))
    u["a"] = swap(u[""], "x1")
    u["b"] = swap(u[""], "y0")
    u["c"] = swap(u[""], "y1")
    b_mate = swap(given, "x0")
    b_sib = swap(integrals, "core")
    u["ab"] = swap(u["b"], "x1")
    u["bc"] = swap(u["c"], "y0")
    u["ac"] = swap(u["a"], "y1")
    rows = [u[n] for n in names[:7]]
    which, slot, partner = lax.optimization_barrier((which, slot, partner))
    own_first, b_own, first = first_product(which, integrals, b_sib, rows[:4])
    cuts = [0, half * 16 // 44 // 128 * 128, half * 32 // 44 // 128 * 128, half]
    cut = [tied(u[n], own_first)[:, cuts[i]:cuts[i + 1]] for i, n in enumerate(("bc", "ac", "ab"))]
    last = jnp.concatenate([swap(t, move) for t, move in zip(cut, ("x1", "y0", "y1"))], axis=1)
    b_mate = tied(b_mate, *cut)
    b_mate_sib = swap(b_mate, "core")
    second = pack([tied(r, *cut) for r in rows[4:]])
    own = [own_first, dot_t(second, b_own), dot_t(last, b_own)]
    b_far = jnp.concatenate([b_mate, b_mate_sib], axis=0)
    mate = [dot_t(t, b_far) for t in (first, second, last)]
    mine, sibling, largest = symmetrize(slot, partner, own, mate)
    sibling = swap(sibling, "core")
    mine = mine + sibling[:total]
    bound = largest[:1] + sibling[total:total + 1]
    power = jnp.clip(14.0 - jnp.ceil(jnp.log2(jnp.maximum(bound, 1e-37))), -120.0, 120.0)
    sent = jnp.concatenate(
        [(mine * jnp.exp2(power)).astype(jnp.float16), jnp.broadcast_to(power.astype(jnp.float16), (16, mine.shape[1]))],
        axis=0)
    came = swap(sent, "x0")
    scale = jnp.exp2(-came[total:total + 1].astype(jnp.float32))
    return came[:total].astype(jnp.float32) * scale + reorder(partner, mine)


def solution(mesh):
    return jax.shard_map(
        shards,
        mesh=mesh,
        in_specs=(P("blk", None), P(("blk", "ab"), None), P(), P()),
        out_specs=P(None, ("blk", "ab")),
        check_vma=False,
    )
```
